512 devices in a mesh: rep: 64 (over z_hi, x, y, core), fsdp: 8 (over z_lo).
Axes of the slice: x: 4, y: 4, z: 16 (z_hi: 2, z_lo: 8; z = z_hi * 8 + z_lo), core: 2. Of those that a mesh axis runs over, the one named last changes fastest.
Arguments:
- tokens: bfloat16 [49152, 4096], P(('rep', 'fsdp')), may hold values from -6 to 6
- norm_gain: float32 [4096], replicated, may hold values from 0.1 to 1.9
- target: bfloat16 [49152, 2, 1024], P('rep', None, 'fsdp'), may hold values from -6 to 6
- master: float32 [2, 4096, 1024], P(None, 'rep', 'fsdp'), may hold values from -0.09375 to 0.09375
- momentum: float32 [2, 4096, 1024], P(None, 'rep', 'fsdp'), may hold values from -4 to 4
Outputs:
- new_master: float32 [2, 4096, 1024], P(None, 'rep', 'fsdp')
- new_momentum: float32 [2, 4096, 1024], P(None, 'rep', 'fsdp')
The draws below stay inside these ranges and needn't reach their ends.
All inputs are finite; a program needn't handle non-finite values.
Results may differ from the reference program's by a relative error of at most 0.00067.
Values may be sent and summed in bfloat16 or wider, within the bound.
A program may use at most 64 MiB of HBM per device.

```python
import jax
import jax.numpy as jnp
from jax import lax

D = 4096
KV = 1024
REP_TOK = 768
TOKENS = 49152
N_REP = 64


def block_levels(own_key, dims, shards, least, largest):
    level, own = 1.0, jax.random.fold_in(own_key, 6)
    for dim, blocks in shards:
        draws = jnp.exp(jax.random.uniform(jax.random.fold_in(own, dim), (blocks,), jnp.float32, least / len(shards), largest / len(shards)))
        level = level * jnp.repeat(draws, dims[dim] // blocks).reshape([-1 if axis == dim else 1 for axis in range(len(dims))])
    return level


def noise(key, extent, width, limit, cuts=(), kind=jnp.bfloat16):
    loudness = block_levels(key, extent, cuts, -0.22, 0.18) if cuts else 1.0
    drawn = jax.random.normal(key, extent, jnp.float32) * width * loudness
    return jnp.minimum(jnp.maximum(drawn, -limit), limit).astype(kind)


def setup_inputs(seed: int = 0) -> dict:
    seeds = jax.random.split(jax.random.key(seed), 6)
    return {
        "tokens": noise(seeds[0], (TOKENS, D), 1.0, 6.0, ((0, 512),)),
        "norm_gain": jnp.clip(1.0 + 0.18 * jax.random.normal(seeds[1], (D,), jnp.float32), 0.1, 1.9),
        "target": noise(seeds[2], (TOKENS, 2, KV), 1.0, 6.0, ((0, 64), (2, 8))),
        "master": noise(seeds[3], (2, D, KV), D ** -0.5, 0.09375, ((1, 64), (2, 8)), jnp.float32),
        "momentum": noise(seeds[4], (2, D, KV), 0.3, 4.0, ((1, 64), (2, 8)), jnp.float32),
    }


inner_rate = 0.02
outer_rate = 0.7
decay_rate = 0.9
norm_eps = 1e-05

def reference(tokens, norm_gain, target, master, momentum):
    values = tokens.astype(jnp.float32)
    scale = lax.rsqrt(lax.optimization_barrier(jnp.mean(values * values, axis=-1, keepdims=True)) + norm_eps)
    normed = (values * scale * norm_gain).astype(jnp.bfloat16)
    weights = master.astype(jnp.bfloat16)
    flat = jnp.transpose(weights, (1, 0, 2)).reshape(D, 2 * KV)
    blocks = normed.reshape(N_REP, REP_TOK, D)
    goals = target.reshape(N_REP, REP_TOK, 2 * KV)

    def one_replica(total, pair):
        rows, goal = pair
        predicted = jnp.dot(rows, flat, preferred_element_type=jnp.float32)
        error = (predicted - goal.astype(jnp.float32)).astype(jnp.bfloat16)
        return (total + jnp.dot(rows.T, error, preferred_element_type=jnp.float32), None)
    total, _ = lax.scan(one_replica, jnp.zeros((D, 2 * KV), jnp.float32), (blocks, goals))
    summed = jnp.transpose(total.reshape(D, 2, KV), (1, 0, 2))
    delta = summed * (inner_rate / N_REP)
    new_momentum = decay_rate * momentum + delta
    new_master = master - outer_rate * (delta + decay_rate * new_momentum)
    return (new_master, new_momentum)
```

```python
import jax
import jax.numpy as jnp
from jax import lax
from jax.experimental import pallas as pl
from jax.experimental.pallas import tpu as pltpu
from jax.sharding import PartitionSpec as P

inner_rate = 0.02
outer_rate = 0.7
decay_rate = 0.9
norm_eps = 1e-05

MESH = pl.DeviceIdType.MESH
NX = 4
NY = 4
LEVELS = 16
HALF = 8
CLASSES = 4
TOK = 96
CHUNKS = 3
ROWS = TOK // CHUNKS
D = 4096
f32 = jnp.float32
bf16 = jnp.bfloat16


def encode(v):
    return (v * jnp.abs(v) * (v * v)).astype(bf16)


def decode(w):
    w = w.astype(f32)
    r = lax.rsqrt(lax.rsqrt(jnp.maximum(jnp.abs(w), 1.2e-38)))
    return jnp.where(w < 0, -r, r)


def kernel(
    tok_ref, gain_ref, tgt_ref, master_ref, mom_ref,
    out_master, out_mom,
    xall, wsh, wg, tg, et, gf, gb, r1a, r1b, af, bfull, a1, b1, r2a, r2b, g3, r3,
    w_send, w_recv, ag1_send, ag1_recv, ag2_send, ag2_recv,
    x1_send, x1_recv, x3_send, x3_recv, x2_send, x2_recv, d_send, d_recv,
    t_send, t_recv, g1_send, g1_recv, g2_send, g2_recv, g3_send, g3_recv,
):
    rep = lax.axis_index("rep")
    lev = lax.axis_index("fsdp")
    core = lax.rem(rep, 2)
    y = lax.rem(rep // 2, NY)
    x = lax.rem(rep // (2 * NY), NX)
    half = rep // (2 * NY * NX)
    z = half * HALF + lev
    cls = lax.rem(lev, CLASSES)
    kt = lev // CLASSES
    col = cls + CLASSES * core
    fdir = 2 * core - 1
    sg = -fdir

    def at(h, xx, yy, c, level):
        return (((h * NX + xx) * NY + yy) * 2 + c, level)

    def at_z(zz, c):
        zz = lax.rem(zz + LEVELS, LEVELS)
        return at(zz // HALF, x, y, c, lax.rem(zz, HALF))

    def rdma(src, dst, ss, rs, dev):
        return pltpu.make_async_remote_copy(
            src_ref=src, dst_ref=dst, send_sem=ss, recv_sem=rs, device_id=dev, device_id_type=MESH
        )

    xpeer = [at(half, lax.rem(x + j, NX), y, core, lev) for j in (1, 2, 3)]
    ypeer = [at(half, x, lax.rem(y + j, NY), core, lev) for j in (1, 2, 3)]
    up = at_z(z + fdir, core)
    down = at_z(z - fdir, core)
    twin = at_z(z, 1 - core)

    barrier = pltpu.get_barrier_semaphore()

    def hello(dev):
        pl.semaphore_signal(barrier, inc=1, device_id=dev, device_id_type=MESH)

    for dev in xpeer + ypeer + [up, down, twin]:
        hello(dev)
    native = lax.rem(kt + core, 2) == 0
    for m in range(4):
        dz = cls + CLASSES * m

        @pl.when(jnp.logical_not(jnp.logical_and(dz == z, native)))
        def _():
            hello(at_z(dz, kt))

        h2, c2 = m // 2, m % 2

        @pl.when(jnp.logical_not(jnp.logical_and(native, jnp.logical_and(h2 == half, c2 == core))))
        def _():
            hello(at(h2, x, y, c2, col))

    gain = gain_ref[...]
    for c in range(CHUNKS):
        v = tok_ref[pl.ds(c * ROWS, ROWS), :].astype(f32)
        scale = lax.rsqrt(jnp.mean(v * v, axis=-1, keepdims=True) + norm_eps)
        xall[pl.ds(c * ROWS, ROWS), :] = (v * scale * gain).astype(bf16)
    wsh[...] = master_ref[...].astype(bf16)

    pl.semaphore_wait(barrier, 9 + 8 - 2 * (1 - lax.rem(kt + core, 2)))

    sidx = half * 2 + core
    wdst = wg.at[:, half, x, y, pl.ds(pl.multiple_of(core * 64, 64), 64), :]

    def w_copy(m):
        return rdma(wsh, wdst, w_send.at[m], w_recv.at[sidx], at_z(cls + CLASSES * m, kt))

    def w_local():
        return pltpu.make_async_copy(wsh, wdst, w_recv.at[sidx])

    for m in range(4):
        mine = jnp.logical_and(cls + CLASSES * m == z, native)

        @pl.when(mine)
        def _():
            w_local().start()

        @pl.when(jnp.logical_not(mine))
        def _():
            w_copy(m).start()

    def slot(s, c, other=False):
        return xall.at[pl.ds((384 if other else 0) + s * TOK + c * ROWS, ROWS), :]

    def x1(c):
        return rdma(slot(0, c), slot(1, c), x1_send.at[c], x1_recv.at[c], up)

    def x3(c):
        return rdma(slot(0, c), slot(3, c), x3_send.at[c], x3_recv.at[c], down)

    def x2(c):
        return rdma(slot(1, c), slot(2, c), x2_send.at[c], x2_recv.at[c], up)

    def to_twin(s, c):
        i = s * CHUNKS + c
        return rdma(slot(s, c), slot(s, c, True), d_send.at[i], d_recv.at[i], twin)

    for c in range(CHUNKS):
        x1(c).start()
        x3(c).start()
    for c in range(CHUNKS):
        to_twin(0, c).start()

    def t_parts(i):
        s = lax.rem(sg * (i - lev) + 8, 4)
        m = s - 4 * (s // 3)
        zt = lax.rem(half * HALF + i - sg * m + LEVELS, LEVELS)
        row = pl.multiple_of((lax.rem(kt + core, 2) * 4 + s) * TOK, TOK)
        idx = lax.rem(kt + core, 2) * 4 + s
        self_ = jnp.logical_and(zt == z, native)
        return tgt_ref.at[:, pl.ds(i * TOK, TOK), :], tg.at[:, pl.ds(row, TOK), :], idx, zt, self_

    for i in range(8):
        src, dst, idx, zt, self_ = t_parts(i)

        @pl.when(self_)
        def _():
            pltpu.make_async_copy(src, dst, t_recv.at[idx]).start()

        @pl.when(jnp.logical_not(self_))
        def _():
            rdma(src, dst, t_send.at[i], t_recv.at[idx], at_z(zt, kt)).start()

    for i in range(4):
        wd = wg.at[:, i // 2, x, y, pl.ds((i % 2) * 64, 64), :]
        rdma(wsh, wd, w_send.at[0], w_recv.at[i], twin).wait_recv()

    def ag1(b, j):
        r = wg.at[b, :, x, y]
        return rdma(r, r, ag1_send.at[b * 3 + j], ag1_recv.at[b * 3 + j], (xpeer if b == 0 else ypeer)[j])

    def ag2(b, j):
        r = wg.at[0, :, :, y] if b == 0 else wg.at[1, :, x]
        return rdma(r, r, ag2_send.at[b * 3 + j], ag2_recv.at[b * 3 + j], (ypeer if b == 0 else xpeer)[j])

    pairs = [(b, j) for j in range(3) for b in range(2)]
    for b, j in pairs:
        ag1(b, j).start()
    for b, j in pairs:
        ag1(b, j).wait_recv()
    for b, j in pairs:
        ag2(b, j).start()

    for c in range(CHUNKS):
        x1(c).wait_recv()
        x2(c).start()
        to_twin(1, c).start()
        x3(c).wait_recv()
        to_twin(3, c).start()
    for c in range(CHUNKS):
        x2(c).wait_recv()
        to_twin(2, c).start()

    for b, j in pairs:
        ag2(b, j).wait_recv()
    for s in (0, 1, 3, 2):
        for c in range(CHUNKS):
            to_twin(s, c).wait_recv()
    for i in range(8):
        dst = tg.at[:, pl.ds(i * TOK, TOK), :]
        rdma(dst, dst, t_send.at[0], t_recv.at[i], twin).wait_recv()

    def forward(i, _):
        r = pl.ds(pl.multiple_of(i * 256, 256), 256)
        w = jnp.concatenate([wg[0].reshape(D, 128), wg[1].reshape(D, 128)], axis=1)
        p = jnp.dot(xall[r, :], w, preferred_element_type=f32)
        goal = jnp.concatenate([tg[0, r, :], tg[1, r, :]], axis=1).astype(f32)
        et[i] = jnp.transpose(p - goal).astype(bf16)
        return 0

    lax.fori_loop(0, 3, forward, 0)

    def backward(t, _):
        cols = pl.ds(pl.multiple_of(t * 512, 512), 512)
        e = jnp.concatenate([et[0], et[1], et[2]], axis=1)
        g = jnp.dot(e, xall[:, cols], preferred_element_type=f32)
        for b in range(2):
            for yy in range(NY):
                piece = g[b * 128:(b + 1) * 128, yy * 128:(yy + 1) * 128]
                gf[b, t // NX, lax.rem(t, NX), yy] = piece
                gb[b, t // NX, lax.rem(t, NX), yy] = encode(piece)
        return 0

    lax.fori_loop(0, 8, backward, 0)

    def g1(b, j):
        if b == 0:
            src, dst = gb.at[0, :, lax.rem(x + j + 1, NX)], r1a.at[j]
        else:
            src, dst = gb.at[1, :, :, lax.rem(y + j + 1, NY)], r1b.at[j]
        return rdma(src, dst, g1_send.at[b * 3 + j], g1_recv.at[b * 3 + j], (xpeer if b == 0 else ypeer)[j])

    for b, j in pairs:
        g1(b, j).start()
    for b, j in pairs:
        g1(b, j).wait_recv()

    def sum1(t, _):
        h, i = t // 4, lax.rem(t, 4)
        va = gf[0, h, x, i] + decode(r1a[0, h, i]) + decode(r1a[1, h, i]) + decode(r1a[2, h, i])
        vb = gf[1, h, i, y] + decode(r1b[0, h, i]) + decode(r1b[1, h, i]) + decode(r1b[2, h, i])
        af[h, i] = va
        bfull[h, i] = vb
        a1[h, i] = encode(va)
        b1[h, i] = encode(vb)
        return 0

    lax.fori_loop(0, 8, sum1, 0)

    def g2(b, j):
        if b == 0:
            src, dst = a1.at[:, lax.rem(y + j + 1, NY)], r2a.at[j]
        else:
            src, dst = b1.at[:, lax.rem(x + j + 1, NX)], r2b.at[j]
        return rdma(src, dst, g2_send.at[b * 3 + j], g2_recv.at[b * 3 + j], (ypeer if b == 0 else xpeer)[j])

    for b, j in pairs:
        g2(b, j).start()
    for b, j in pairs:
        g2(b, j).wait_recv()
    for h in range(2):
        va = af[h, y] + decode(r2a[0, h]) + decode(r2a[1, h]) + decode(r2a[2, h])
        vb = bfull[h, x] + decode(r2b[0, h]) + decode(r2b[1, h]) + decode(r2b[2, h])
        g3[h, 0] = encode(jnp.transpose(va))
        g3[h, 1] = encode(jnp.transpose(vb))

    m_own = z // CLASSES

    def g3_parts(i):
        h2, c2 = i // 2, i % 2
        src = g3.at[h2, :, pl.ds(c2 * 64, 64), :]
        self_ = jnp.logical_and(native, jnp.logical_and(half == h2, core == c2))
        return src, r3.at[m_own], at(h2, x, y, c2, col), self_

    for i in range(4):
        src, dst, dev, self_ = g3_parts(i)

        @pl.when(self_)
        def _():
            pltpu.make_async_copy(src, dst, g3_recv.at[m_own]).start()

        @pl.when(jnp.logical_not(self_))
        def _():
            rdma(src, dst, g3_send.at[i], g3_recv.at[m_own], dev).start()

    for i in range(4):
        rdma(r3.at[i], r3.at[i], g3_send.at[0], g3_recv.at[i], twin).wait_recv()

    total = decode(r3[0]) + decode(r3[1]) + decode(r3[2]) + decode(r3[3])
    delta = total * (inner_rate / 64)
    new_mom = decay_rate * mom_ref[...] + delta
    out_mom[...] = new_mom
    out_master[...] = master_ref[...] - outer_rate * (delta + decay_rate * new_mom)

    for m in range(4):
        @pl.when(jnp.logical_not(jnp.logical_and(cls + CLASSES * m == z, native)))
        def _():
            w_copy(m).wait_send()
    for c in range(CHUNKS):
        x1(c).wait_send()
        x2(c).wait_send()
        x3(c).wait_send()
        for s in range(4):
            to_twin(s, c).wait_send()
    for i in range(8):
        src, dst, idx, zt, self_ = t_parts(i)

        @pl.when(jnp.logical_not(self_))
        def _():
            rdma(src, dst, t_send.at[i], t_recv.at[idx], at_z(zt, kt)).wait_send()
    for b, j in pairs:
        ag1(b, j).wait_send()
        ag2(b, j).wait_send()
        g1(b, j).wait_send()
        g2(b, j).wait_send()
    for i in range(4):
        src, dst, dev, self_ = g3_parts(i)

        @pl.when(jnp.logical_not(self_))
        def _():
            rdma(src, dst, g3_send.at[i], g3_recv.at[m_own], dev).wait_send()


def body(tokens, norm_gain, target, master, momentum):
    goal = jnp.transpose(target, (1, 0, 2))
    vm = pl.BlockSpec(memory_space=pltpu.VMEM)
    dma = pltpu.SemaphoreType.DMA
    shard = jax.ShapeDtypeStruct(master.shape, f32)
    V = pltpu.VMEM
    scratch = [
        V((768, D), bf16),
        V((2, 64, 128), bf16),
        V((2, 2, NX, NY, 128, 128), bf16),
        V((2, 768, 128), bf16),
        V((3, 256, 256), bf16),
        V((2, 2, NX, NY, 128, 128), f32),
        V((2, 2, NX, NY, 128, 128), bf16),
        V((3, 2, NY, 128, 128), bf16),
        V((3, 2, NX, 128, 128), bf16),
        V((2, NY, 128, 128), f32),
        V((2, NX, 128, 128), f32),
        V((2, NY, 128, 128), bf16),
        V((2, NX, 128, 128), bf16),
        V((3, 2, 128, 128), bf16),
        V((3, 2, 128, 128), bf16),
        V((2, 2, 128, 128), bf16),
        V((4, 2, 64, 128), bf16),
        dma((4,)), dma((4,)), dma((6,)), dma((6,)), dma((6,)), dma((6,)),
        dma((CHUNKS,)), dma((CHUNKS,)), dma((CHUNKS,)), dma((CHUNKS,)), dma((CHUNKS,)), dma((CHUNKS,)),
        dma((4 * CHUNKS,)), dma((4 * CHUNKS,)),
        dma((8,)), dma((8,)), dma((6,)), dma((6,)), dma((6,)), dma((6,)), dma((4,)), dma((4,)),
    ]
    return pl.pallas_call(
        kernel,
        out_shape=(shard, shard),
        in_specs=[vm] * 5,
        out_specs=(vm, vm),
        scratch_shapes=scratch,
        compiler_params=pltpu.CompilerParams(
            collective_id=0, has_side_effects=True, vmem_limit_bytes=48 * 1024 * 1024
        ),
        cost_estimate=pl.CostEstimate(flops=3_300_000_000, bytes_accessed=2_000_000, transcendentals=0),
    )(tokens, norm_gain.reshape(1, D), goal, master, momentum)


def solution(mesh):
    in_specs = (
        P(("rep", "fsdp"), None),
        P(),
        P("rep", None, "fsdp"),
        P(None, "rep", "fsdp"),
        P(None, "rep", "fsdp"),
    )
    out_specs = (P(None, "rep", "fsdp"), P(None, "rep", "fsdp"))
    return jax.shard_map(body, mesh=mesh, in_specs=in_specs, out_specs=out_specs, check_vma=False)
```

```python
import jax
import jax.numpy as jnp
from jax import lax
from jax.experimental import pallas as pl
from jax.experimental.pallas import tpu as pltpu
from jax.sharding import PartitionSpec as P

inner_rate = 0.02
outer_rate = 0.7
decay_rate = 0.9
norm_eps = 1e-05

MESH = pl.DeviceIdType.MESH
NX = 4
NY = 4
LEVELS = 16
HALF = 8
CLASSES = 4
TOK = 96
CHUNKS = 3
ROWS = TOK // CHUNKS
D = 4096
f32 = jnp.float32
bf16 = jnp.bfloat16


def encode(v):
    return (v * jnp.abs(v) * (v * v)).astype(bf16)


def decode(w):
    w = w.astype(f32)
    r = lax.rsqrt(lax.rsqrt(jnp.maximum(jnp.abs(w), 1.2e-38)))
    return jnp.where(w < 0, -r, r)


def kernel(
    tok_ref, gain_ref, goal_ref, master_ref,
    out_ref,
    xin, gain, mst, xall, wsh, wg, tg, pred, et, own, gb, r1, mid, a1, r2, g3, r3,
    in_sem, w_send, w_recv, ag1_send, ag1_recv, ag2_send, ag2_recv,
    x1_send, x1_recv, x3_send, x3_recv, x2_send, x2_recv, d_send, d_recv,
    t_send, t_recv, g1_send, g1_recv, g2_send, g2_recv, g3_send, g3_recv,
):
    loads = [
        pltpu.make_async_copy(src, dst, in_sem.at[i])
        for i, (src, dst) in enumerate(((tok_ref, xin), (gain_ref, gain), (master_ref, mst)))
    ]
    for load in loads:
        load.start()

    rep = lax.axis_index("rep")
    lev = lax.axis_index("fsdp")
    core = lax.rem(rep, 2)
    y = lax.rem(rep // 2, NY)
    x = lax.rem(rep // (2 * NY), NX)
    half = rep // (2 * NY * NX)
    z = half * HALF + lev
    cls = lax.rem(lev, CLASSES)
    kt = lev // CLASSES
    col = cls + CLASSES * core
    fdir = 2 * core - 1
    sg = -fdir
    foreign = lax.rem(kt + core, 2)
    native = foreign == 0

    def at(h, xx, yy, c, level):
        return (((h * NX + xx) * NY + yy) * 2 + c, level)

    def at_z(zz, c):
        zz = lax.rem(zz + LEVELS, LEVELS)
        return at(zz // HALF, x, y, c, lax.rem(zz, HALF))

    def rdma(src, dst, ss, rs, dev):
        return pltpu.make_async_remote_copy(
            src_ref=src, dst_ref=dst, send_sem=ss, recv_sem=rs, device_id=dev, device_id_type=MESH
        )

    xpeer = [at(half, lax.rem(x + j, NX), y, core, lev) for j in (1, 2, 3)]
    ypeer = [at(half, x, lax.rem(y + j, NY), core, lev) for j in (1, 2, 3)]
    up = at_z(z + fdir, core)
    down = at_z(z - fdir, core)
    twin = at_z(z, 1 - core)

    barrier = pltpu.get_barrier_semaphore()

    def hello(dev):
        pl.semaphore_signal(barrier, inc=1, device_id=dev, device_id_type=MESH)

    for dev in xpeer + ypeer + [up, down, twin]:
        hello(dev)
    for m in range(4):
        dz = cls + CLASSES * m

        @pl.when(jnp.logical_not(jnp.logical_and(dz == z, native)))
        def _():
            hello(at_z(dz, kt))

        h2, c2 = m // 2, m % 2

        @pl.when(jnp.logical_not(jnp.logical_and(native, jnp.logical_and(h2 == half, c2 == core))))
        def _():
            hello(at(h2, x, y, c2, col))

    for load in loads:
        load.wait()
    wsh[...] = mst[...].astype(bf16)
    for c in range(CHUNKS):
        v = xin[pl.ds(c * ROWS, ROWS), :].astype(f32)
        scale = lax.rsqrt(jnp.mean(v * v, axis=-1, keepdims=True) + norm_eps)
        xall[pl.ds(c * ROWS, ROWS), :] = (v * scale * gain[...]).astype(bf16)

    pl.semaphore_wait(barrier, 9 + 8 - 2 * (1 - foreign))

    sidx = half * 2 + core
    wdst = wg.at[:, half, x, y, pl.ds(pl.multiple_of(core * 64, 64), 64), :]

    def w_copy(m):
        return rdma(wsh, wdst, w_send.at[m], w_recv.at[sidx], at_z(cls + CLASSES * m, kt))

    for m in range(4):
        mine = jnp.logical_and(cls + CLASSES * m == z, native)

        @pl.when(mine)
        def _():
            pltpu.make_async_copy(wsh, wdst, w_recv.at[sidx]).start()

        @pl.when(jnp.logical_not(mine))
        def _():
            w_copy(m).start()

    base = ((0, 96, 576, 192), (288, 384, 672, 480))

    def slot(s, c, other=0):
        return xall.at[pl.ds(base[other][s] + c * ROWS, ROWS), :]

    def x1(c):
        return rdma(slot(0, c), slot(1, c), x1_send.at[c], x1_recv.at[c], up)

    def x3(c):
        return rdma(slot(0, c), slot(3, c), x3_send.at[c], x3_recv.at[c], down)

    def x2(c):
        return rdma(slot(1, c), slot(2, c), x2_send.at[c], x2_recv.at[c], up)

    def to_twin(s, c):
        i = s * CHUNKS + c
        return rdma(slot(s, c), slot(s, c, 1), d_send.at[i], d_recv.at[i], twin)

    for c in range(CHUNKS):
        x1(c).start()
        x3(c).start()
    for c in range(CHUNKS):
        to_twin(0, c).start()

    def t_parts(kv, i):
        s = lax.rem(sg * (i - lev) + 8, 4)
        m = s - 4 * (s // 3)
        zt = lax.rem(half * HALF + i - sg * m + LEVELS, LEVELS)
        last = s // 2 - s // 3
        row = last * (576 + TOK * foreign) + (1 - last) * (288 * foreign + TOK * (s - s // 3))
        row = pl.multiple_of(row, TOK)
        idx = kv * 8 + foreign * 4 + s
        self_ = jnp.logical_and(zt == z, native)
        return goal_ref.at[kv, pl.ds(i * TOK, TOK), :], tg.at[kv, pl.ds(row, TOK), :], idx, zt, self_

    def send_targets(kv):
        for i in range(8):
            src, dst, idx, zt, self_ = t_parts(kv, i)

            @pl.when(self_)
            def _():
                pltpu.make_async_copy(src, dst, t_recv.at[idx]).start()

            @pl.when(jnp.logical_not(self_))
            def _():
                rdma(src, dst, t_send.at[kv * 8 + i], t_recv.at[idx], at_z(zt, kt)).start()

    send_targets(0)

    for i in range(4):
        wd = wg.at[:, i // 2, x, y, pl.ds((i % 2) * 64, 64), :]
        rdma(wsh, wd, w_send.at[0], w_recv.at[i], twin).wait_recv()

    def ag1(b, j):
        r = wg.at[b, :, x, y]
        return rdma(r, r, ag1_send.at[b * 3 + j], ag1_recv.at[b * 3 + j], (xpeer if b == 0 else ypeer)[j])

    def ag2(b, j):
        r = wg.at[0, :, :, y] if b == 0 else wg.at[1, :, x]
        return rdma(r, r, ag2_send.at[b * 3 + j], ag2_recv.at[b * 3 + j], (ypeer if b == 0 else xpeer)[j])

    pairs = [(b, j) for j in range(3) for b in range(2)]
    for b, j in pairs:
        ag1(b, j).start()
    for b, j in pairs:
        ag1(b, j).wait_recv()
    for b, j in pairs:
        ag2(b, j).start()

    for c in range(CHUNKS):
        x1(c).wait_recv()
        x2(c).start()
        to_twin(1, c).start()
        x3(c).wait_recv()
        to_twin(3, c).start()

    for b, j in pairs:
        ag2(b, j).wait_recv()
    for s in (0, 1, 3):
        for c in range(CHUNKS):
            to_twin(s, c).wait_recv()

    def forward(first, rows):
        w = jnp.concatenate([wg[0].reshape(D, 128), wg[1].reshape(D, 128)], axis=1)
        p = jnp.dot(xall[pl.ds(first, rows), :], w, preferred_element_type=f32)
        for kv in range(2):
            pred[kv, pl.ds(first, rows), :] = p[:, kv * 128:(kv + 1) * 128]

    def early(i, _):
        forward(pl.multiple_of(i * 288, 32), 288)
        return 0

    lax.fori_loop(0, 2, early, 0)
    for c in range(CHUNKS):
        x2(c).wait_recv()
        to_twin(2, c).start()
    send_targets(1)
    for c in range(CHUNKS):
        to_twin(2, c).wait_recv()
    forward(576, 192)

    first = (x, y)
    second = (y, x)
    peer1 = (xpeer, ypeer)
    peer2 = (ypeer, xpeer)

    def sem1(kv, ab, j):
        return (kv * 2 + ab) * 3 + j

    def g1(kv, ab, j):
        i = sem1(kv, ab, j)
        return rdma(gb.at[kv, ab, j], r1.at[kv, ab, j], g1_send.at[i], g1_recv.at[i], peer1[ab][j])

    def backward(kv):
        for i in range(8):
            dst = tg.at[kv, pl.ds(i * TOK, TOK), :]
            rdma(dst, dst, t_send.at[0], t_recv.at[kv * 8 + i], twin).wait_recv()
        et[kv] = jnp.transpose(pred[kv] - tg[kv].astype(f32)).astype(bf16)
        for j in range(4):
            for ab in range(2):
                t = lax.rem(first[ab] + j + 1, 4)
                if ab == 0:
                    block = xall[:, pl.ds(pl.multiple_of(t * 512, 512), 512)]
                else:
                    block = jnp.concatenate(
                        [xall[:, pl.ds(pl.multiple_of(2048 + i * 512 + t * 128, 128), 128)] for i in range(4)], axis=1
                    )
                g = jnp.dot(et[kv], block, preferred_element_type=f32)
                for i in range(4):
                    piece = g[:, i * 128:(i + 1) * 128]
                    if j < 3:
                        gb[kv, ab, j, i] = encode(piece)
                    else:
                        own[kv, ab, i] = piece
                if j < 3:
                    g1(kv, ab, j).start()

    def g2(kv, ab, j):
        i = sem1(kv, ab, j)
        return rdma(a1.at[kv, ab, j], r2.at[kv, ab, j], g2_send.at[i], g2_recv.at[i], peer2[ab][j])

    def sum1(kv):
        for ab in range(2):
            for j in range(3):
                g1(kv, ab, j).wait_recv()
        for j in range(4):
            for ab in range(2):
                i = lax.rem(second[ab] + j + 1, 4)
                v = own[kv, ab, i]
                for n in range(3):
                    v = v + decode(r1[kv, ab, n, i])
                if j < 3:
                    a1[kv, ab, j] = encode(v)
                    g2(kv, ab, j).start()
                else:
                    mid[kv, ab] = v

    m_own = z // CLASSES

    def g3_parts(kv, i):
        h2, c2 = i // 2, i % 2
        src = g3.at[kv, h2, pl.ds(c2 * 64, 64), :]
        self_ = jnp.logical_and(native, jnp.logical_and(half == h2, core == c2))
        return src, r3.at[kv, m_own], kv * 4 + m_own, at(h2, x, y, c2, col), self_

    def sum2(kv):
        for ab in range(2):
            for j in range(3):
                g2(kv, ab, j).wait_recv()
            v = mid[kv, ab]
            for n in range(3):
                v = v + decode(r2[kv, ab, n])
            g3[kv, ab] = encode(jnp.transpose(v))
            for i in (2 * ab, 2 * ab + 1):
                src, dst, idx, dev, self_ = g3_parts(kv, i)

                @pl.when(self_)
                def _():
                    pltpu.make_async_copy(src, dst, g3_recv.at[idx]).start()

                @pl.when(jnp.logical_not(self_))
                def _():
                    rdma(src, dst, g3_send.at[kv * 4 + i], g3_recv.at[idx], dev).start()

    def finish(kv):
        for i in range(4):
            rdma(r3.at[kv, i], r3.at[kv, i], g3_send.at[0], g3_recv.at[kv * 4 + i], twin).wait_recv()
        out_ref[kv] = (decode(r3[kv, 0]) + decode(r3[kv, 1])) + (decode(r3[kv, 2]) + decode(r3[kv, 3]))

    backward(0)
    backward(1)
    sum1(0)
    sum2(0)
    sum1(1)
    finish(0)
    sum2(1)
    finish(1)

    for m in range(4):
        @pl.when(jnp.logical_not(jnp.logical_and(cls + CLASSES * m == z, native)))
        def _():
            w_copy(m).wait_send()
    for c in range(CHUNKS):
        x1(c).wait_send()
        x2(c).wait_send()
        x3(c).wait_send()
        for s in range(4):
            to_twin(s, c).wait_send()
    for b, j in pairs:
        ag1(b, j).wait_send()
        ag2(b, j).wait_send()
    for kv in range(2):
        for i in range(8):
            src, dst, idx, zt, self_ = t_parts(kv, i)

            @pl.when(jnp.logical_not(self_))
            def _():
                rdma(src, dst, t_send.at[kv * 8 + i], t_recv.at[idx], at_z(zt, kt)).wait_send()
        for ab in range(2):
            for j in range(3):
                g1(kv, ab, j).wait_send()
                g2(kv, ab, j).wait_send()
        for i in range(4):
            src, dst, idx, dev, self_ = g3_parts(kv, i)

            @pl.when(jnp.logical_not(self_))
            def _():
                rdma(src, dst, g3_send.at[kv * 4 + i], g3_recv.at[idx], dev).wait_send()


def body(tokens, norm_gain, target, master, momentum):
    goal = jnp.transpose(target, (1, 0, 2))
    hbm = pl.BlockSpec(memory_space=pltpu.HBM)
    dma = pltpu.SemaphoreType.DMA
    V = pltpu.VMEM
    scratch = [
        V((TOK, D), bf16),
        V((1, D), f32),
        V((2, 64, 128), f32),
        V((768, D), bf16),
        V((2, 64, 128), bf16),
        V((2, 2, NX, NY, 128, 128), bf16),
        V((2, 768, 128), bf16),
        V((2, 768, 128), f32),
        V((2, 128, 768), bf16),
        V((2, 2, 4, 128, 128), f32),
        V((2, 2, 3, 4, 128, 128), bf16),
        V((2, 2, 3, 4, 128, 128), bf16),
        V((2, 2, 128, 128), f32),
        V((2, 2, 3, 128, 128), bf16),
        V((2, 2, 3, 128, 128), bf16),
        V((2, 2, 128, 128), bf16),
        V((2, 4, 64, 128), bf16),
        dma((3,)), dma((4,)), dma((4,)), dma((6,)), dma((6,)), dma((6,)), dma((6,)),
        dma((CHUNKS,)), dma((CHUNKS,)), dma((CHUNKS,)), dma((CHUNKS,)), dma((CHUNKS,)), dma((CHUNKS,)),
        dma((4 * CHUNKS,)), dma((4 * CHUNKS,)),
        dma((16,)), dma((16,)), dma((12,)), dma((12,)), dma((12,)), dma((12,)), dma((8,)), dma((8,)),
    ]
    summed = pl.pallas_call(
        kernel,
        out_shape=jax.ShapeDtypeStruct(master.shape, f32),
        in_specs=[hbm] * 4,
        out_specs=pl.BlockSpec(memory_space=pltpu.VMEM),
        scratch_shapes=scratch,
        compiler_params=pltpu.CompilerParams(
            collective_id=0, has_side_effects=True, vmem_limit_bytes=63 * 1024 * 1024
        ),
        cost_estimate=pl.CostEstimate(flops=3_300_000_000, bytes_accessed=2_000_000, transcendentals=0),
    )(tokens, norm_gain.reshape(1, D), goal, master)
    delta = summed * (inner_rate / 64)
    new_momentum = decay_rate * momentum + delta
    new_master = master - outer_rate * (delta + decay_rate * new_momentum)
    return (new_master, new_momentum)


def solution(mesh):
    in_specs = (
        P(("rep", "fsdp"), None),
        P(),
        P("rep", None, "fsdp"),
        P(None, "rep", "fsdp"),
        P(None, "rep", "fsdp"),
    )
    out_specs = (P(None, "rep", "fsdp"), P(None, "rep", "fsdp"))
    return jax.shard_map(body, mesh=mesh, in_specs=in_specs, out_specs=out_specs, check_vma=False)
```

```python
import jax
import jax.numpy as jnp
from jax import lax
from jax.experimental import pallas as pl
from jax.experimental.pallas import tpu as pltpu
from jax.sharding import PartitionSpec as P

inner_rate = 0.02
outer_rate = 0.7
decay_rate = 0.9
norm_eps = 1e-05

MESH = pl.DeviceIdType.MESH
NX = 4
NY = 4
LEVELS = 16
HALF = 8
CLASSES = 4
TOK = 96
CHUNKS = 3
ROWS = TOK // CHUNKS
D = 4096
f32 = jnp.float32
bf16 = jnp.bfloat16


def encode(v):
    return (v * jnp.abs(v) * (v * v)).astype(bf16)


def decode(w):
    w = w.astype(f32)
    r = lax.rsqrt(lax.rsqrt(jnp.maximum(jnp.abs(w), 1.2e-38)))
    return jnp.where(w < 0, -r, r)


def kernel(
    tok_ref, gain_ref, tgt_ref, master_ref,
    out_ref,
    xin, gain, mst, tin, goal, raw, xall, wsh, wg, tg, pred, et, own, gb, r1, mid, a1, r2, g3, r3,
    in_sem, w_send, w_recv, ag1_send, ag1_recv, ag2_send, ag2_recv,
    x1_send, x1_recv, x3_send, x3_recv, x2_send, x2_recv, d_send, d_recv,
    t_send, t_recv, g1_send, g1_recv, g2_send, g2_recv, g3_send, g3_recv,
):
    loads = [
        pltpu.make_async_copy(src, dst, in_sem.at[i])
        for i, (src, dst) in enumerate(((master_ref, mst), (tok_ref, xin), (gain_ref, gain), (tgt_ref, tin)))
    ]
    for load in loads:
        load.start()

    rep = lax.axis_index("rep")
    lev = lax.axis_index("fsdp")
    core = lax.rem(rep, 2)
    y = lax.rem(rep // 2, NY)
    x = lax.rem(rep // (2 * NY), NX)
    half = rep // (2 * NY * NX)
    z = half * HALF + lev
    cls = lax.rem(lev, CLASSES)
    kt = lev // CLASSES
    col = cls + CLASSES * core
    fdir = 2 * core - 1
    sg = -fdir
    foreign = lax.rem(kt + core, 2)
    native = foreign == 0

    def at(h, xx, yy, c, level):
        return (((h * NX + xx) * NY + yy) * 2 + c, level)

    def at_z(zz, c):
        zz = lax.rem(zz + LEVELS, LEVELS)
        return at(zz // HALF, x, y, c, lax.rem(zz, HALF))

    def rdma(src, dst, ss, rs, dev):
        return pltpu.make_async_remote_copy(
            src_ref=src, dst_ref=dst, send_sem=ss, recv_sem=rs, device_id=dev, device_id_type=MESH
        )

    xpeer = [at(half, lax.rem(x + j, NX), y, core, lev) for j in (1, 2, 3)]
    ypeer = [at(half, x, lax.rem(y + j, NY), core, lev) for j in (1, 2, 3)]
    up = at_z(z + fdir, core)
    down = at_z(z - fdir, core)
    twin = at_z(z, 1 - core)

    barrier = pltpu.get_barrier_semaphore()

    def hello(dev):
        pl.semaphore_signal(barrier, inc=1, device_id=dev, device_id_type=MESH)

    for dev in xpeer + ypeer + [up, down, twin]:
        hello(dev)
    for m in range(4):
        dz = cls + CLASSES * m

        @pl.when(jnp.logical_not(jnp.logical_and(dz == z, native)))
        def _():
            hello(at_z(dz, kt))

        h2, c2 = m // 2, m % 2

        @pl.when(jnp.logical_not(jnp.logical_and(native, jnp.logical_and(h2 == half, c2 == core))))
        def _():
            hello(at(h2, x, y, c2, col))

    loads[0].wait()
    wsh[...] = mst[...].astype(bf16)

    pl.semaphore_wait(barrier, 9 + 8 - 2 * (1 - foreign))

    sidx = half * 2 + core
    wdst = wg.at[:, half, x, y, pl.ds(pl.multiple_of(core * 64, 64), 64), :]

    def w_copy(m):
        return rdma(wsh, wdst, w_send.at[m], w_recv.at[sidx], at_z(cls + CLASSES * m, kt))

    for m in range(4):
        mine = jnp.logical_and(cls + CLASSES * m == z, native)

        @pl.when(mine)
        def _():
            pltpu.make_async_copy(wsh, wdst, w_recv.at[sidx]).start()

        @pl.when(jnp.logical_not(mine))
        def _():
            w_copy(m).start()

    base = ((0, 96, 576, 192), (288, 384, 672, 480))

    def slot(s, c, other=0):
        return xall.at[pl.ds(base[other][s] + c * ROWS, ROWS), :]

    def x1(c):
        return rdma(tok_ref.at[pl.ds(c * ROWS, ROWS), :], raw.at[0, c], x1_send.at[c], x1_recv.at[c], up)

    def x3(c):
        return rdma(tok_ref.at[pl.ds(c * ROWS, ROWS), :], raw.at[1, c], x3_send.at[c], x3_recv.at[c], down)

    def x2(c):
        return rdma(slot(1, c), slot(2, c), x2_send.at[c], x2_recv.at[c], up)

    def to_twin(s, c):
        i = s * CHUNKS + c
        return rdma(slot(s, c), slot(s, c, 1), d_send.at[i], d_recv.at[i], twin)

    def norm(v, s, c):
        v = v.astype(f32)
        scale = lax.rsqrt(jnp.mean(v * v, axis=-1, keepdims=True) + norm_eps)
        slot(s, c)[...] = (v * scale * gain[...]).astype(bf16)

    for c in range(CHUNKS):
        x1(c).start()
    for c in range(CHUNKS):
        x3(c).start()
    loads[1].wait()
    loads[2].wait()
    for c in range(CHUNKS):
        norm(xin[pl.ds(c * ROWS, ROWS), :], 0, c)
        to_twin(0, c).start()
    loads[3].wait()
    for i in range(8):
        rows = pl.ds(i * TOK, TOK)
        goal[:, rows, :] = jnp.swapaxes(tin[rows], 0, 1)

    def t_parts(kv, i):
        s = lax.rem(sg * (i - lev) + 8, 4)
        m = s - 4 * (s // 3)
        zt = lax.rem(half * HALF + i - sg * m + LEVELS, LEVELS)
        last = s // 2 - s // 3
        row = last * (576 + TOK * foreign) + (1 - last) * (288 * foreign + TOK * (s - s // 3))
        row = pl.multiple_of(row, TOK)
        idx = kv * 8 + foreign * 4 + s
        self_ = jnp.logical_and(zt == z, native)
        return goal.at[kv, pl.ds(i * TOK, TOK), :], tg.at[kv, pl.ds(row, TOK), :], idx, zt, self_

    def send_targets(kv):
        for i in range(8):
            src, dst, idx, zt, self_ = t_parts(kv, i)

            @pl.when(self_)
            def _():
                pltpu.make_async_copy(src, dst, t_recv.at[idx]).start()

            @pl.when(jnp.logical_not(self_))
            def _():
                rdma(src, dst, t_send.at[kv * 8 + i], t_recv.at[idx], at_z(zt, kt)).start()

    send_targets(0)

    for i in range(4):
        wd = wg.at[:, i // 2, x, y, pl.ds((i % 2) * 64, 64), :]
        rdma(wsh, wd, w_send.at[0], w_recv.at[i], twin).wait_recv()

    def ag1(b, j):
        r = wg.at[b, :, x, y]
        return rdma(r, r, ag1_send.at[b * 3 + j], ag1_recv.at[b * 3 + j], (xpeer if b == 0 else ypeer)[j])

    def ag2(b, j):
        r = wg.at[0, :, :, y] if b == 0 else wg.at[1, :, x]
        return rdma(r, r, ag2_send.at[b * 3 + j], ag2_recv.at[b * 3 + j], (ypeer if b == 0 else xpeer)[j])

    pairs = [(b, j) for j in range(3) for b in range(2)]
    for b, j in pairs:
        ag1(b, j).start()
    for b, j in pairs:
        ag1(b, j).wait_recv()
    for b, j in pairs:
        ag2(b, j).start()

    for c in range(CHUNKS):
        x1(c).wait_recv()
        norm(raw[0, c], 1, c)
        x2(c).start()
        to_twin(1, c).start()
    for c in range(CHUNKS):
        x3(c).wait_recv()
        norm(raw[1, c], 3, c)
        to_twin(3, c).start()

    for b, j in pairs:
        ag2(b, j).wait_recv()
    for s in (0, 1, 3):
        for c in range(CHUNKS):
            to_twin(s, c).wait_recv()

    def forward(first, rows):
        w = jnp.concatenate([wg[0].reshape(D, 128), wg[1].reshape(D, 128)], axis=1)
        p = jnp.dot(xall[pl.ds(first, rows), :], w, preferred_element_type=f32)
        for kv in range(2):
            pred[kv, pl.ds(first, rows), :] = p[:, kv * 128:(kv + 1) * 128]

    def early(i, _):
        forward(pl.multiple_of(i * 288, 32), 288)
        return 0

    lax.fori_loop(0, 2, early, 0)
    for c in range(CHUNKS):
        x2(c).wait_recv()
        to_twin(2, c).start()
    send_targets(1)
    for c in range(CHUNKS):
        to_twin(2, c).wait_recv()
    forward(576, 192)

    first = (x, y)
    second = (y, x)
    peer1 = (xpeer, ypeer)
    peer2 = (ypeer, xpeer)

    def g1(kv, ab, n, j):
        i = ((kv * 2 + ab) * 4 + n) * 3 + j
        return rdma(gb.at[kv, ab, n, j], r1.at[kv, ab, n, j], g1_send.at[i], g1_recv.at[i], peer1[ab][j])

    def backward(kv):
        for i in range(8):
            dst = tg.at[kv, pl.ds(i * TOK, TOK), :]
            rdma(dst, dst, t_send.at[0], t_recv.at[kv * 8 + i], twin).wait_recv()
        et[kv] = jnp.transpose(pred[kv] - tg[kv].astype(f32)).astype(bf16)
        for n in range(4):
            for ab in range(2):
                i = lax.rem(second[ab] + n + 1, 4)
                ts = [lax.rem(first[ab] + j + 1, 4) for j in range(4)]
                starts = [(t * 512 + i * 128) if ab == 0 else (2048 + i * 512 + t * 128) for t in ts]
                block = jnp.concatenate([xall[:, pl.ds(pl.multiple_of(c0, 128), 128)] for c0 in starts], axis=1)
                g = jnp.dot(et[kv], block, preferred_element_type=f32)
                for j in range(3):
                    gb[kv, ab, n, j] = encode(g[:, j * 128:(j + 1) * 128])
                    g1(kv, ab, n, j).start()
                own[kv, ab, n] = g[:, 384:]

    def g2(kv, ab, j):
        i = (kv * 2 + ab) * 3 + j
        return rdma(a1.at[kv, ab, j], r2.at[kv, ab, j], g2_send.at[i], g2_recv.at[i], peer2[ab][j])

    def sum1(kv):
        for n in range(4):
            for ab in range(2):
                v = own[kv, ab, n]
                for j in range(3):
                    g1(kv, ab, n, j).wait_recv()
                    v = v + decode(r1[kv, ab, n, j])
                if n < 3:
                    a1[kv, ab, n] = encode(v)
                    g2(kv, ab, n).start()
                else:
                    mid[kv, ab] = v

    m_own = z // CLASSES

    def g3_parts(kv, i):
        h2, c2 = i // 2, i % 2
        src = g3.at[kv, h2, pl.ds(c2 * 64, 64), :]
        self_ = jnp.logical_and(native, jnp.logical_and(half == h2, core == c2))
        return src, r3.at[kv, m_own], kv * 4 + m_own, at(h2, x, y, c2, col), self_

    def sum2(kv):
        for ab in range(2):
            for j in range(3):
                g2(kv, ab, j).wait_recv()
            v = mid[kv, ab]
            for n in range(3):
                v = v + decode(r2[kv, ab, n])
            g3[kv, ab] = encode(jnp.transpose(v))
            for i in (2 * ab, 2 * ab + 1):
                src, dst, idx, dev, self_ = g3_parts(kv, i)

                @pl.when(self_)
                def _():
                    pltpu.make_async_copy(src, dst, g3_recv.at[idx]).start()

                @pl.when(jnp.logical_not(self_))
                def _():
                    rdma(src, dst, g3_send.at[kv * 4 + i], g3_recv.at[idx], dev).start()

    def finish(kv):
        for i in range(4):
            rdma(r3.at[kv, i], r3.at[kv, i], g3_send.at[0], g3_recv.at[kv * 4 + i], twin).wait_recv()
        out_ref[kv] = (decode(r3[kv, 0]) + decode(r3[kv, 1])) + (decode(r3[kv, 2]) + decode(r3[kv, 3]))

    backward(0)
    backward(1)
    sum1(0)
    sum1(1)
    sum2(0)
    sum2(1)
    finish(0)
    finish(1)

    for m in range(4):
        @pl.when(jnp.logical_not(jnp.logical_and(cls + CLASSES * m == z, native)))
        def _():
            w_copy(m).wait_send()
    for c in range(CHUNKS):
        x1(c).wait_send()
        x2(c).wait_send()
        x3(c).wait_send()
        for s in range(4):
            to_twin(s, c).wait_send()
    for b, j in pairs:
        ag1(b, j).wait_send()
        ag2(b, j).wait_send()
    for kv in range(2):
        for i in range(8):
            src, dst, idx, zt, self_ = t_parts(kv, i)

            @pl.when(jnp.logical_not(self_))
            def _():
                rdma(src, dst, t_send.at[kv * 8 + i], t_recv.at[idx], at_z(zt, kt)).wait_send()
        for ab in range(2):
            for j in range(3):
                g2(kv, ab, j).wait_send()
                for n in range(4):
                    g1(kv, ab, n, j).wait_send()
        for i in range(4):
            src, dst, idx, dev, self_ = g3_parts(kv, i)

            @pl.when(jnp.logical_not(self_))
            def _():
                rdma(src, dst, g3_send.at[kv * 4 + i], g3_recv.at[idx], dev).wait_send()


def body(tokens, norm_gain, target, master, momentum):
    hbm = pl.BlockSpec(memory_space=pltpu.HBM)
    dma = pltpu.SemaphoreType.DMA
    V = pltpu.VMEM
    scratch = [
        V((TOK, D), bf16),
        V((1, D), f32),
        V((2, 64, 128), f32),
        V((768, 2, 128), bf16),
        V((2, 768, 128), bf16),
        V((2, CHUNKS, ROWS, D), bf16),
        V((768, D), bf16),
        V((2, 64, 128), bf16),
        V((2, 2, NX, NY, 128, 128), bf16),
        V((2, 768, 128), bf16),
        V((2, 768, 128), f32),
        V((2, 128, 768), bf16),
        V((2, 2, 4, 128, 128), f32),
        V((2, 2, 4, 3, 128, 128), bf16),
        V((2, 2, 4, 3, 128, 128), bf16),
        V((2, 2, 128, 128), f32),
        V((2, 2, 3, 128, 128), bf16),
        V((2, 2, 3, 128, 128), bf16),
        V((2, 2, 128, 128), bf16),
        V((2, 4, 64, 128), bf16),
        dma((4,)), dma((4,)), dma((4,)), dma((6,)), dma((6,)), dma((6,)), dma((6,)),
        dma((CHUNKS,)), dma((CHUNKS,)), dma((CHUNKS,)), dma((CHUNKS,)), dma((CHUNKS,)), dma((CHUNKS,)),
        dma((4 * CHUNKS,)), dma((4 * CHUNKS,)),
        dma((16,)), dma((16,)), dma((48,)), dma((48,)), dma((12,)), dma((12,)), dma((8,)), dma((8,)),
    ]
    summed = pl.pallas_call(
        kernel,
        out_shape=jax.ShapeDtypeStruct(master.shape, f32),
        in_specs=[hbm] * 4,
        out_specs=pl.BlockSpec(memory_space=pltpu.VMEM),
        scratch_shapes=scratch,
        compiler_params=pltpu.CompilerParams(
            collective_id=0, has_side_effects=True, vmem_limit_bytes=60 * 1024 * 1024
        ),
        cost_estimate=pl.CostEstimate(flops=3_300_000_000, bytes_accessed=2_000_000, transcendentals=0),
    )(tokens, norm_gain.reshape(1, D), target, master)
    delta = summed * (inner_rate / 64)
    new_momentum = decay_rate * momentum + delta
    new_master = master - outer_rate * (delta + decay_rate * new_momentum)
    return (new_master, new_momentum)


def solution(mesh):
    in_specs = (
        P(("rep", "fsdp"), None),
        P(),
        P("rep", None, "fsdp"),
        P(None, "rep", "fsdp"),
        P(None, "rep", "fsdp"),
    )
    out_specs = (P(None, "rep", "fsdp"), P(None, "rep", "fsdp"))
    return jax.shard_map(body, mesh=mesh, in_specs=in_specs, out_specs=out_specs, check_vma=False)
```

```python
import jax
import jax.numpy as jnp
from jax import lax
from jax.experimental import pallas as pl
from jax.experimental.pallas import tpu as pltpu
from jax.sharding import PartitionSpec as P

inner_rate = 0.02
outer_rate = 0.7
decay_rate = 0.9
norm_eps = 1e-05

MESH = pl.DeviceIdType.MESH
NX = 4
NY = 4
LEVELS = 16
HALF = 8
CLASSES = 4
FAR_FIRST = (2, 1, 3, 4)
TOK = 96
CHUNKS = 2
ROWS = TOK // CHUNKS
D = 4096
f32 = jnp.float32
bf16 = jnp.bfloat16


def encode(v):
    return (v * jnp.abs(v) * (v * v)).astype(bf16)


def decode(w):
    w = w.astype(f32)
    r = lax.rsqrt(lax.rsqrt(jnp.maximum(jnp.abs(w), 1.2e-38)))
    return jnp.where(w < 0, -r, r)


def kernel(
    tok_ref, gain_ref, tgt_ref, master_ref,
    out_ref,
    xin, gain, mst, tin, goal, raw, xall, wsh, wg, tg, pred, et, own, gb, r1, mid, a1, r2, g3, r3,
    in_sem, w_send, w_recv, ag1_send, ag1_recv, ag2_send, ag2_recv,
    x1_send, x1_recv, x3_send, x3_recv, x2_send, x2_recv, d_send, d_recv,
    t_send, t_recv, g1_send, g1_recv, g2_send, g2_recv, g3_send, g3_recv,
):
    loads = [
        pltpu.make_async_copy(src, dst, in_sem.at[i])
        for i, (src, dst) in enumerate(((master_ref, mst), (tok_ref, xin), (gain_ref, gain), (tgt_ref, tin)))
    ]
    for load in loads:
        load.start()

    rep = lax.axis_index("rep")
    lev = lax.axis_index("fsdp")
    core = lax.rem(rep, 2)
    y = lax.rem(rep // 2, NY)
    x = lax.rem(rep // (2 * NY), NX)
    half = rep // (2 * NY * NX)
    z = half * HALF + lev
    cls = lax.rem(lev, CLASSES)
    kt = lev // CLASSES
    col = cls + CLASSES * core
    fdir = 2 * core - 1
    sg = -fdir
    foreign = lax.rem(kt + core, 2)
    native = foreign == 0

    def at(h, xx, yy, c, level):
        return (((h * NX + xx) * NY + yy) * 2 + c, level)

    def at_z(zz, c):
        zz = lax.rem(zz + LEVELS, LEVELS)
        return at(zz // HALF, x, y, c, lax.rem(zz, HALF))

    def rdma(src, dst, ss, rs, dev):
        return pltpu.make_async_remote_copy(
            src_ref=src, dst_ref=dst, send_sem=ss, recv_sem=rs, device_id=dev, device_id_type=MESH
        )

    xpeer = [at(half, lax.rem(x + j, NX), y, core, lev) for j in FAR_FIRST[:3]]
    ypeer = [at(half, x, lax.rem(y + j, NY), core, lev) for j in FAR_FIRST[:3]]
    up = at_z(z + fdir, core)
    down = at_z(z - fdir, core)
    twin = at_z(z, 1 - core)

    barrier = pltpu.get_barrier_semaphore()

    def hello(dev):
        pl.semaphore_signal(barrier, inc=1, device_id=dev, device_id_type=MESH)

    for dev in xpeer + ypeer + [up, down, twin]:
        hello(dev)
    for m in range(4):
        dz = cls + CLASSES * m

        @pl.when(jnp.logical_not(jnp.logical_and(dz == z, native)))
        def _():
            hello(at_z(dz, kt))

        h2, c2 = m // 2, m % 2

        @pl.when(jnp.logical_not(jnp.logical_and(native, jnp.logical_and(h2 == half, c2 == core))))
        def _():
            hello(at(h2, x, y, c2, col))

    loads[0].wait()
    wsh[...] = mst[...].astype(bf16)

    pl.semaphore_wait(barrier, 9 + 8 - 2 * (1 - foreign))

    sidx = half * 2 + core
    wdst = wg.at[:, half, x, y, pl.ds(pl.multiple_of(core * 64, 64), 64), :]

    def w_copy(m):
        return rdma(wsh, wdst, w_send.at[m], w_recv.at[sidx], at_z(cls + CLASSES * m, kt))

    for m in range(4):
        mine = jnp.logical_and(cls + CLASSES * m == z, native)

        @pl.when(mine)
        def _():
            pltpu.make_async_copy(wsh, wdst, w_recv.at[sidx]).start()

        @pl.when(jnp.logical_not(mine))
        def _():
            w_copy(m).start()

    base = ((0, 96, 576, 192), (288, 384, 672, 480))

    def slot(s, c, other=0):
        return xall.at[pl.ds(base[other][s] + c * ROWS, ROWS), :]

    def x1(c):
        return rdma(tok_ref.at[pl.ds(c * ROWS, ROWS), :], raw.at[0, c], x1_send.at[c], x1_recv.at[c], up)

    def x3(c):
        return rdma(tok_ref.at[pl.ds(c * ROWS, ROWS), :], raw.at[1, c], x3_send.at[c], x3_recv.at[c], down)

    def x2(c):
        return rdma(slot(1, c), slot(2, c), x2_send.at[c], x2_recv.at[c], up)

    def to_twin(s, c):
        i = s * CHUNKS + c
        return rdma(slot(s, c), slot(s, c, 1), d_send.at[i], d_recv.at[i], twin)

    def norm(v, s, c):
        v = v.astype(f32)
        scale = lax.rsqrt(jnp.mean(v * v, axis=-1, keepdims=True) + norm_eps)
        slot(s, c)[...] = (v * scale * gain[...]).astype(bf16)

    for c in range(CHUNKS):
        x1(c).start()
    for c in range(CHUNKS):
        x3(c).start()
    loads[1].wait()
    loads[2].wait()
    for c in range(CHUNKS):
        norm(xin[pl.ds(c * ROWS, ROWS), :], 0, c)
        to_twin(0, c).start()
    loads[3].wait()
    for i in range(8):
        rows = pl.ds(i * TOK, TOK)
        goal[:, rows, :] = jnp.swapaxes(tin[rows], 0, 1)

    def t_parts(kv, i):
        s = lax.rem(sg * (i - lev) + 8, 4)
        m = s - 4 * (s // 3)
        zt = lax.rem(half * HALF + i - sg * m + LEVELS, LEVELS)
        last = s // 2 - s // 3
        row = last * (576 + TOK * foreign) + (1 - last) * (288 * foreign + TOK * (s - s // 3))
        row = pl.multiple_of(row, TOK)
        idx = kv * 8 + foreign * 4 + s
        self_ = jnp.logical_and(zt == z, native)
        return goal.at[kv, pl.ds(i * TOK, TOK), :], tg.at[kv, pl.ds(row, TOK), :], idx, zt, self_

    def send_targets(kv):
        for i in range(8):
            src, dst, idx, zt, self_ = t_parts(kv, i)

            @pl.when(self_)
            def _():
                pltpu.make_async_copy(src, dst, t_recv.at[idx]).start()

            @pl.when(jnp.logical_not(self_))
            def _():
                rdma(src, dst, t_send.at[kv * 8 + i], t_recv.at[idx], at_z(zt, kt)).start()

    send_targets(0)

    for i in range(4):
        wd = wg.at[:, i // 2, x, y, pl.ds((i % 2) * 64, 64), :]
        rdma(wsh, wd, w_send.at[0], w_recv.at[i], twin).wait_recv()

    def ag1(b, j):
        r = wg.at[b, :, x, y]
        return rdma(r, r, ag1_send.at[b * 3 + j], ag1_recv.at[b * 3 + j], (xpeer if b == 0 else ypeer)[j])

    def ag2(b, j):
        r = wg.at[0, :, :, y] if b == 0 else wg.at[1, :, x]
        return rdma(r, r, ag2_send.at[b * 3 + j], ag2_recv.at[b * 3 + j], (ypeer if b == 0 else xpeer)[j])

    pairs = [(b, j) for j in range(3) for b in range(2)]
    for b, j in pairs:
        ag1(b, j).start()
    for b, j in pairs:
        ag1(b, j).wait_recv()
    for b, j in pairs:
        ag2(b, j).start()

    for c in range(CHUNKS):
        x1(c).wait_recv()
        norm(raw[0, c], 1, c)
        x2(c).start()
        to_twin(1, c).start()
    for c in range(CHUNKS):
        x3(c).wait_recv()
        norm(raw[1, c], 3, c)
        to_twin(3, c).start()

    for b, j in pairs:
        ag2(b, j).wait_recv()
    for s in (0, 1, 3):
        for c in range(CHUNKS):
            to_twin(s, c).wait_recv()

    def forward(first, rows):
        w = jnp.concatenate([wg[0].reshape(D, 128), wg[1].reshape(D, 128)], axis=1)
        p = jnp.dot(xall[pl.ds(first, rows), :], w, preferred_element_type=f32)
        for kv in range(2):
            pred[kv, pl.ds(first, rows), :] = p[:, kv * 128:(kv + 1) * 128]

    def early(i, _):
        forward(pl.multiple_of(i * 288, 32), 288)
        return 0

    lax.fori_loop(0, 2, early, 0)
    for c in range(CHUNKS):
        x2(c).wait_recv()
        to_twin(2, c).start()
    send_targets(1)
    for c in range(CHUNKS):
        to_twin(2, c).wait_recv()
    forward(576, 192)

    first = (x, y)
    second = (y, x)
    peer1 = (xpeer, ypeer)
    peer2 = (ypeer, xpeer)

    def g1(kv, ab, n, j):
        i = ((kv * 2 + ab) * 4 + n) * 3 + j
        return rdma(gb.at[kv, ab, n, j], r1.at[kv, ab, n, j], g1_send.at[i], g1_recv.at[i], peer1[ab][j])

    def backward(kv):
        for i in range(8):
            dst = tg.at[kv, pl.ds(i * TOK, TOK), :]
            rdma(dst, dst, t_send.at[0], t_recv.at[kv * 8 + i], twin).wait_recv()
        et[kv] = jnp.transpose(pred[kv] - tg[kv].astype(f32)).astype(bf16)
        for n in range(4):
            for ab in range(2):
                i = lax.rem(second[ab] + FAR_FIRST[n], 4)
                ts = [lax.rem(first[ab] + j, 4) for j in FAR_FIRST]
                starts = [(t * 512 + i * 128) if ab == 0 else (2048 + i * 512 + t * 128) for t in ts]
                block = jnp.concatenate([xall[:, pl.ds(pl.multiple_of(c0, 128), 128)] for c0 in starts], axis=1)
                g = jnp.dot(et[kv], block, preferred_element_type=f32)
                for j in range(3):
                    gb[kv, ab, n, j] = encode(g[:, j * 128:(j + 1) * 128])
                    g1(kv, ab, n, j).start()
                own[kv, ab, n] = g[:, 384:]

    def g2(kv, ab, j):
        i = (kv * 2 + ab) * 3 + j
        return rdma(a1.at[kv, ab, j], r2.at[kv, ab, j], g2_send.at[i], g2_recv.at[i], peer2[ab][j])

    def sum1(kv):
        for n in range(4):
            for ab in range(2):
                v = own[kv, ab, n]
                for j in range(3):
                    g1(kv, ab, n, j).wait_recv()
                    v = v + decode(r1[kv, ab, n, j])
                if n < 3:
                    a1[kv, ab, n] = encode(v)
                    g2(kv, ab, n).start()
                else:
                    mid[kv, ab] = v

    m_own = z // CLASSES

    def g3_parts(kv, i):
        h2, c2 = i // 2, i % 2
        src = g3.at[kv, h2, pl.ds(c2 * 64, 64), :]
        self_ = jnp.logical_and(native, jnp.logical_and(half == h2, core == c2))
        return src, r3.at[kv, m_own], kv * 4 + m_own, at(h2, x, y, c2, col), self_

    def sum2(kv):
        for ab in range(2):
            for j in range(3):
                g2(kv, ab, j).wait_recv()
            v = mid[kv, ab]
            for n in range(3):
                v = v + decode(r2[kv, ab, n])
            g3[kv, ab] = encode(jnp.transpose(v))
            for i in (2 * ab, 2 * ab + 1):
                src, dst, idx, dev, self_ = g3_parts(kv, i)

                @pl.when(self_)
                def _():
                    pltpu.make_async_copy(src, dst, g3_recv.at[idx]).start()

                @pl.when(jnp.logical_not(self_))
                def _():
                    rdma(src, dst, g3_send.at[kv * 4 + i], g3_recv.at[idx], dev).start()

    def finish(kv):
        for i in range(4):
            rdma(r3.at[kv, i], r3.at[kv, i], g3_send.at[0], g3_recv.at[kv * 4 + i], twin).wait_recv()
        out_ref[kv] = (decode(r3[kv, 0]) + decode(r3[kv, 1])) + (decode(r3[kv, 2]) + decode(r3[kv, 3]))

    backward(0)
    backward(1)
    sum1(0)
    sum1(1)
    sum2(0)
    sum2(1)
    finish(0)
    finish(1)

    for m in range(4):
        @pl.when(jnp.logical_not(jnp.logical_and(cls + CLASSES * m == z, native)))
        def _():
            w_copy(m).wait_send()
    for c in range(CHUNKS):
        x1(c).wait_send()
        x2(c).wait_send()
        x3(c).wait_send()
        for s in range(4):
            to_twin(s, c).wait_send()
    for b, j in pairs:
        ag1(b, j).wait_send()
        ag2(b, j).wait_send()
    for kv in range(2):
        for i in range(8):
            src, dst, idx, zt, self_ = t_parts(kv, i)

            @pl.when(jnp.logical_not(self_))
            def _():
                rdma(src, dst, t_send.at[kv * 8 + i], t_recv.at[idx], at_z(zt, kt)).wait_send()
        for ab in range(2):
            for j in range(3):
                g2(kv, ab, j).wait_send()
                for n in range(4):
                    g1(kv, ab, n, j).wait_send()
        for i in range(4):
            src, dst, idx, dev, self_ = g3_parts(kv, i)

            @pl.when(jnp.logical_not(self_))
            def _():
                rdma(src, dst, g3_send.at[kv * 4 + i], g3_recv.at[idx], dev).wait_send()


def body(tokens, norm_gain, target, master, momentum):
    hbm = pl.BlockSpec(memory_space=pltpu.HBM)
    dma = pltpu.SemaphoreType.DMA
    V = pltpu.VMEM
    scratch = [
        V((TOK, D), bf16),
        V((1, D), f32),
        V((2, 64, 128), f32),
        V((768, 2, 128), bf16),
        V((2, 768, 128), bf16),
        V((2, CHUNKS, ROWS, D), bf16),
        V((768, D), bf16),
        V((2, 64, 128), bf16),
        V((2, 2, NX, NY, 128, 128), bf16),
        V((2, 768, 128), bf16),
        V((2, 768, 128), f32),
        V((2, 128, 768), bf16),
        V((2, 2, 4, 128, 128), f32),
        V((2, 2, 4, 3, 128, 128), bf16),
        V((2, 2, 4, 3, 128, 128), bf16),
        V((2, 2, 128, 128), f32),
        V((2, 2, 3, 128, 128), bf16),
        V((2, 2, 3, 128, 128), bf16),
        V((2, 2, 128, 128), bf16),
        V((2, 4, 64, 128), bf16),
        dma((4,)), dma((4,)), dma((4,)), dma((6,)), dma((6,)), dma((6,)), dma((6,)),
        dma((CHUNKS,)), dma((CHUNKS,)), dma((CHUNKS,)), dma((CHUNKS,)), dma((CHUNKS,)), dma((CHUNKS,)),
        dma((4 * CHUNKS,)), dma((4 * CHUNKS,)),
        dma((16,)), dma((16,)), dma((48,)), dma((48,)), dma((12,)), dma((12,)), dma((8,)), dma((8,)),
    ]
    summed = pl.pallas_call(
        kernel,
        out_shape=jax.ShapeDtypeStruct(master.shape, f32),
        in_specs=[hbm] * 4,
        out_specs=pl.BlockSpec(memory_space=pltpu.VMEM),
        scratch_shapes=scratch,
        compiler_params=pltpu.CompilerParams(
            collective_id=0, has_side_effects=True, vmem_limit_bytes=60 * 1024 * 1024
        ),
        cost_estimate=pl.CostEstimate(flops=3_300_000_000, bytes_accessed=2_000_000, transcendentals=0),
    )(tokens, norm_gain.reshape(1, D), target, master)
    delta = summed * (inner_rate / 64)
    new_momentum = decay_rate * momentum + delta
    new_master = master - outer_rate * (delta + decay_rate * new_momentum)
    return (new_master, new_momentum)


def solution(mesh):
    in_specs = (
        P(("rep", "fsdp"), None),
        P(),
        P("rep", None, "fsdp"),
        P(None, "rep", "fsdp"),
        P(None, "rep", "fsdp"),
    )
    out_specs = (P(None, "rep", "fsdp"), P(None, "rep", "fsdp"))
    return jax.shard_map(body, mesh=mesh, in_specs=in_specs, out_specs=out_specs, check_vma=False)
```

```python
import jax
import jax.numpy as jnp
from jax import lax
from jax.experimental import pallas as pl
from jax.experimental.pallas import tpu as pltpu
from jax.sharding import PartitionSpec as P

inner_rate = 0.02
outer_rate = 0.7
decay_rate = 0.9
norm_eps = 1e-05

MESH = pl.DeviceIdType.MESH
NX = 4
NY = 4
LEVELS = 16
HALF = 8
CLASSES = 4
FAR_FIRST = (2, 1, 3, 4)
TOK = 96
CHUNKS = 2
ROWS = TOK // CHUNKS
D = 4096
f32 = jnp.float32
bf16 = jnp.bfloat16


def encode(v):
    return (v * jnp.abs(v) * (v * v)).astype(bf16)


def decode(w):
    w = w.astype(f32)
    r = lax.rsqrt(lax.rsqrt(jnp.maximum(jnp.abs(w), 1.2e-38)))
    return jnp.where(w < 0, -r, r)


def kernel(
    tok_ref, gain_ref, tgt_ref, master_ref,
    out_ref,
    xin, gain, mst, tin, goal, raw, xall, wsh, wg, tg, pred, et, own, gb, r1, mid, a1, r2, g3, r3,
    in_sem, w_send, w_recv, ag1_send, ag1_recv, ag2_send, ag2_recv,
    x1_send, x1_recv, x3_send, x3_recv, x2_send, x2_recv, d_send, d_recv,
    t_send, t_recv, g1_send, g1_recv, g2_send, g2_recv, g3_send, g3_recv,
):
    loads = [
        pltpu.make_async_copy(src, dst, in_sem.at[i])
        for i, (src, dst) in enumerate(((master_ref, mst), (tok_ref, xin), (gain_ref, gain), (tgt_ref, tin)))
    ]
    for load in loads:
        load.start()

    rep = lax.axis_index("rep")
    lev = lax.axis_index("fsdp")
    core = lax.rem(rep, 2)
    y = lax.rem(rep // 2, NY)
    x = lax.rem(rep // (2 * NY), NX)
    half = rep // (2 * NY * NX)
    z = half * HALF + lev
    cls = lax.rem(lev, CLASSES)
    kt = lev // CLASSES
    col = cls + CLASSES * core
    fdir = 2 * core - 1
    sg = -fdir
    foreign = lax.rem(kt + core, 2)
    native = foreign == 0

    def at(h, xx, yy, c, level):
        return (((h * NX + xx) * NY + yy) * 2 + c, level)

    def at_z(zz, c):
        zz = lax.rem(zz + LEVELS, LEVELS)
        return at(zz // HALF, x, y, c, lax.rem(zz, HALF))

    def rdma(src, dst, ss, rs, dev):
        return pltpu.make_async_remote_copy(
            src_ref=src, dst_ref=dst, send_sem=ss, recv_sem=rs, device_id=dev, device_id_type=MESH
        )

    xpeer = [at(half, lax.rem(x + j, NX), y, core, lev) for j in FAR_FIRST[:3]]
    ypeer = [at(half, x, lax.rem(y + j, NY), core, lev) for j in FAR_FIRST[:3]]
    up = at_z(z + fdir, core)
    down = at_z(z - fdir, core)
    twin = at_z(z, 1 - core)

    barrier = pltpu.get_barrier_semaphore()

    def hello(dev):
        pl.semaphore_signal(barrier, inc=1, device_id=dev, device_id_type=MESH)

    for dev in xpeer + ypeer + [up, down, twin]:
        hello(dev)
    for m in range(4):
        dz = cls + CLASSES * m

        @pl.when(jnp.logical_not(jnp.logical_and(dz == z, native)))
        def _():
            hello(at_z(dz, kt))

        h2, c2 = m // 2, m % 2

        @pl.when(jnp.logical_not(jnp.logical_and(native, jnp.logical_and(h2 == half, c2 == core))))
        def _():
            hello(at(h2, x, y, c2, col))

    loads[0].wait()
    wsh[...] = mst[...].astype(bf16)

    pl.semaphore_wait(barrier, 9 + 8 - 2 * (1 - foreign))

    sidx = half * 2 + core
    wdst = wg.at[:, half, x, y, pl.ds(pl.multiple_of(core * 64, 64), 64), :]

    def w_copy(m):
        return rdma(wsh, wdst, w_send.at[m], w_recv.at[sidx], at_z(cls + CLASSES * m, kt))

    for m in range(4):
        mine = jnp.logical_and(cls + CLASSES * m == z, native)

        @pl.when(mine)
        def _():
            pltpu.make_async_copy(wsh, wdst, w_recv.at[sidx]).start()

        @pl.when(jnp.logical_not(mine))
        def _():
            w_copy(m).start()

    base = ((0, 96, 576, 192), (288, 384, 672, 480))

    def slot(s, c, other=0):
        return xall.at[pl.ds(base[other][s] + c * ROWS, ROWS), :]

    def x1(c):
        return rdma(tok_ref.at[pl.ds(c * ROWS, ROWS), :], raw.at[0, c], x1_send.at[c], x1_recv.at[c], up)

    def x3(c):
        return rdma(tok_ref.at[pl.ds(c * ROWS, ROWS), :], raw.at[1, c], x3_send.at[c], x3_recv.at[c], down)

    def x2(c):
        return rdma(slot(1, c), slot(2, c), x2_send.at[c], x2_recv.at[c], up)

    def to_twin(s, c):
        i = s * CHUNKS + c
        return rdma(slot(s, c), slot(s, c, 1), d_send.at[i], d_recv.at[i], twin)

    def norm(v, s, c):
        v = v.astype(f32)
        scale = lax.rsqrt(jnp.mean(v * v, axis=-1, keepdims=True) + norm_eps)
        slot(s, c)[...] = (v * scale * gain[...]).astype(bf16)

    for c in range(CHUNKS):
        x1(c).start()
    for c in range(CHUNKS):
        x3(c).start()
    loads[1].wait()
    loads[2].wait()
    for c in range(CHUNKS):
        norm(xin[pl.ds(c * ROWS, ROWS), :], 0, c)
        to_twin(0, c).start()
    loads[3].wait()
    for i in range(8):
        rows = pl.ds(i * TOK, TOK)
        goal[:, rows, :] = jnp.swapaxes(tin[rows], 0, 1)

    def t_parts(kv, i):
        s = lax.rem(sg * (i - lev) + 8, 4)
        m = s - 4 * (s // 3)
        zt = lax.rem(half * HALF + i - sg * m + LEVELS, LEVELS)
        last = s // 2 - s // 3
        row = last * (576 + TOK * foreign) + (1 - last) * (288 * foreign + TOK * (s - s // 3))
        row = pl.multiple_of(row, TOK)
        idx = kv * 8 + foreign * 4 + s
        self_ = jnp.logical_and(zt == z, native)
        return goal.at[kv, pl.ds(i * TOK, TOK), :], tg.at[kv, pl.ds(row, TOK), :], idx, zt, self_

    def send_targets(kv):
        for i in (0, 7, 1, 6, 2, 5, 3, 4):
            src, dst, idx, zt, self_ = t_parts(kv, i)

            @pl.when(self_)
            def _():
                pltpu.make_async_copy(src, dst, t_recv.at[idx]).start()

            @pl.when(jnp.logical_not(self_))
            def _():
                rdma(src, dst, t_send.at[kv * 8 + i], t_recv.at[idx], at_z(zt, kt)).start()

    send_targets(0)

    for i in range(4):
        wd = wg.at[:, i // 2, x, y, pl.ds((i % 2) * 64, 64), :]
        rdma(wsh, wd, w_send.at[0], w_recv.at[i], twin).wait_recv()

    def ag1(b, j):
        r = wg.at[b, :, x, y]
        return rdma(r, r, ag1_send.at[b * 3 + j], ag1_recv.at[b * 3 + j], (xpeer if b == 0 else ypeer)[j])

    def ag2(b, j):
        r = wg.at[0, :, :, y] if b == 0 else wg.at[1, :, x]
        return rdma(r, r, ag2_send.at[b * 3 + j], ag2_recv.at[b * 3 + j], (ypeer if b == 0 else xpeer)[j])

    pairs = [(b, j) for j in range(3) for b in range(2)]
    for b, j in pairs:
        ag1(b, j).start()
    for b, j in pairs:
        ag1(b, j).wait_recv()
    for b, j in pairs:
        ag2(b, j).start()

    for c in range(CHUNKS):
        x1(c).wait_recv()
        norm(raw[0, c], 1, c)
        x2(c).start()
        to_twin(1, c).start()
    for c in range(CHUNKS):
        x3(c).wait_recv()
        norm(raw[1, c], 3, c)
        to_twin(3, c).start()

    for b, j in pairs:
        ag2(b, j).wait_recv()
    for s in (0, 1, 3):
        for c in range(CHUNKS):
            to_twin(s, c).wait_recv()

    def forward(first, rows):
        w = jnp.concatenate([wg[0].reshape(D, 128), wg[1].reshape(D, 128)], axis=1)
        p = jnp.dot(xall[pl.ds(first, rows), :], w, preferred_element_type=f32)
        for kv in range(2):
            pred[kv, pl.ds(first, rows), :] = p[:, kv * 128:(kv + 1) * 128]

    def early(i, _):
        forward(pl.multiple_of(i * 288, 32), 288)
        return 0

    lax.fori_loop(0, 2, early, 0)
    for c in range(CHUNKS):
        x2(c).wait_recv()
        to_twin(2, c).start()
    send_targets(1)
    for c in range(CHUNKS):
        to_twin(2, c).wait_recv()
    forward(576, 192)

    first = (x, y)
    second = (y, x)
    peer1 = (xpeer, ypeer)
    peer2 = (ypeer, xpeer)

    def g1(kv, ab, n, j):
        i = ((kv * 2 + ab) * 4 + n) * 3 + j
        return rdma(gb.at[kv, ab, n, j], r1.at[kv, ab, n, j], g1_send.at[i], g1_recv.at[i], peer1[ab][j])

    def backward(kv):
        for i in range(8):
            dst = tg.at[kv, pl.ds(i * TOK, TOK), :]
            rdma(dst, dst, t_send.at[0], t_recv.at[kv * 8 + i], twin).wait_recv()
        et[kv] = jnp.transpose(pred[kv] - tg[kv].astype(f32)).astype(bf16)
        for n in range(4):
            for ab in range(2):
                i = lax.rem(second[ab] + FAR_FIRST[n], 4)
                ts = [lax.rem(first[ab] + j, 4) for j in FAR_FIRST]
                starts = [(t * 512 + i * 128) if ab == 0 else (2048 + i * 512 + t * 128) for t in ts]
                block = jnp.concatenate([xall[:, pl.ds(pl.multiple_of(c0, 128), 128)] for c0 in starts], axis=1)
                g = jnp.dot(et[kv], block, preferred_element_type=f32)
                for j in range(3):
                    gb[kv, ab, n, j] = encode(g[:, j * 128:(j + 1) * 128])
                    g1(kv, ab, n, j).start()
                own[kv, ab, n] = g[:, 384:]

    def g2(kv, ab, j):
        i = (kv * 2 + ab) * 3 + j
        return rdma(a1.at[kv, ab, j], r2.at[kv, ab, j], g2_send.at[i], g2_recv.at[i], peer2[ab][j])

    def sum1(kv):
        for n in range(4):
            for ab in range(2):
                v = own[kv, ab, n]
                for j in range(3):
                    g1(kv, ab, n, j).wait_recv()
                    v = v + decode(r1[kv, ab, n, j])
                if n < 3:
                    a1[kv, ab, n] = encode(v)
                    g2(kv, ab, n).start()
                else:
                    mid[kv, ab] = v

    m_own = z // CLASSES

    def g3_parts(kv, i):
        h2, c2 = i // 2, i % 2
        src = g3.at[kv, h2, pl.ds(c2 * 64, 64), :]
        self_ = jnp.logical_and(native, jnp.logical_and(half == h2, core == c2))
        return src, r3.at[kv, m_own], kv * 4 + m_own, at(h2, x, y, c2, col), self_

    def sum2(kv):
        for ab in range(2):
            for j in range(3):
                g2(kv, ab, j).wait_recv()
            v = mid[kv, ab]
            for n in range(3):
                v = v + decode(r2[kv, ab, n])
            g3[kv, ab] = encode(jnp.transpose(v))
            for i in (2 * ab, 2 * ab + 1):
                src, dst, idx, dev, self_ = g3_parts(kv, i)

                @pl.when(self_)
                def _():
                    pltpu.make_async_copy(src, dst, g3_recv.at[idx]).start()

                @pl.when(jnp.logical_not(self_))
                def _():
                    rdma(src, dst, g3_send.at[kv * 4 + i], g3_recv.at[idx], dev).start()

    def finish(kv):
        for i in range(4):
            rdma(r3.at[kv, i], r3.at[kv, i], g3_send.at[0], g3_recv.at[kv * 4 + i], twin).wait_recv()
        out_ref[kv] = (decode(r3[kv, 0]) + decode(r3[kv, 1])) + (decode(r3[kv, 2]) + decode(r3[kv, 3]))

    backward(0)
    backward(1)
    sum1(0)
    sum1(1)
    sum2(0)
    sum2(1)
    finish(0)
    finish(1)

    for m in range(4):
        @pl.when(jnp.logical_not(jnp.logical_and(cls + CLASSES * m == z, native)))
        def _():
            w_copy(m).wait_send()
    for c in range(CHUNKS):
        x1(c).wait_send()
        x2(c).wait_send()
        x3(c).wait_send()
        for s in range(4):
            to_twin(s, c).wait_send()
    for b, j in pairs:
        ag1(b, j).wait_send()
        ag2(b, j).wait_send()
    for kv in range(2):
        for i in range(8):
            src, dst, idx, zt, self_ = t_parts(kv, i)

            @pl.when(jnp.logical_not(self_))
            def _():
                rdma(src, dst, t_send.at[kv * 8 + i], t_recv.at[idx], at_z(zt, kt)).wait_send()
        for ab in range(2):
            for j in range(3):
                g2(kv, ab, j).wait_send()
                for n in range(4):
                    g1(kv, ab, n, j).wait_send()
        for i in range(4):
            src, dst, idx, dev, self_ = g3_parts(kv, i)

            @pl.when(jnp.logical_not(self_))
            def _():
                rdma(src, dst, g3_send.at[kv * 4 + i], g3_recv.at[idx], dev).wait_send()


def body(tokens, norm_gain, target, master, momentum):
    hbm = pl.BlockSpec(memory_space=pltpu.HBM)
    dma = pltpu.SemaphoreType.DMA
    V = pltpu.VMEM
    scratch = [
        V((TOK, D), bf16),
        V((1, D), f32),
        V((2, 64, 128), f32),
        V((768, 2, 128), bf16),
        V((2, 768, 128), bf16),
        V((2, CHUNKS, ROWS, D), bf16),
        V((768, D), bf16),
        V((2, 64, 128), bf16),
        V((2, 2, NX, NY, 128, 128), bf16),
        V((2, 768, 128), bf16),
        V((2, 768, 128), f32),
        V((2, 128, 768), bf16),
        V((2, 2, 4, 128, 128), f32),
        V((2, 2, 4, 3, 128, 128), bf16),
        V((2, 2, 4, 3, 128, 128), bf16),
        V((2, 2, 128, 128), f32),
        V((2, 2, 3, 128, 128), bf16),
        V((2, 2, 3, 128, 128), bf16),
        V((2, 2, 128, 128), bf16),
        V((2, 4, 64, 128), bf16),
        dma((4,)), dma((4,)), dma((4,)), dma((6,)), dma((6,)), dma((6,)), dma((6,)),
        dma((CHUNKS,)), dma((CHUNKS,)), dma((CHUNKS,)), dma((CHUNKS,)), dma((CHUNKS,)), dma((CHUNKS,)),
        dma((4 * CHUNKS,)), dma((4 * CHUNKS,)),
        dma((16,)), dma((16,)), dma((48,)), dma((48,)), dma((12,)), dma((12,)), dma((8,)), dma((8,)),
    ]
    summed = pl.pallas_call(
        kernel,
        out_shape=jax.ShapeDtypeStruct(master.shape, f32),
        in_specs=[hbm] * 4,
        out_specs=pl.BlockSpec(memory_space=pltpu.VMEM),
        scratch_shapes=scratch,
        compiler_params=pltpu.CompilerParams(
            collective_id=0, has_side_effects=True, vmem_limit_bytes=60 * 1024 * 1024
        ),
        cost_estimate=pl.CostEstimate(flops=3_300_000_000, bytes_accessed=2_000_000, transcendentals=0),
    )(tokens, norm_gain.reshape(1, D), target, master)
    delta = summed * (inner_rate / 64)
    new_momentum = decay_rate * momentum + delta
    new_master = master - outer_rate * (delta + decay_rate * new_momentum)
    return (new_master, new_momentum)


def solution(mesh):
    in_specs = (
        P(("rep", "fsdp"), None),
        P(),
        P("rep", None, "fsdp"),
        P(None, "rep", "fsdp"),
        P(None, "rep", "fsdp"),
    )
    out_specs = (P(None, "rep", "fsdp"), P(None, "rep", "fsdp"))
    return jax.shard_map(body, mesh=mesh, in_specs=in_specs, out_specs=out_specs, check_vma=False)
```
